32 devices in a mesh: members: 2 (over y), lat: 8 (over z, x), lon: 2 (over core).
Axes of the slice: x: 2, y: 2, z: 4, core: 2. Of those that a mesh axis runs over, the one named last changes fastest.
Arguments:
- state: float32 [16, 32, 256], P('members', 'lat', 'lon'), parts along dimension 0, may hold values from -6 to 6
- tangents: float32 [64, 8, 32, 256], P('members', None, 'lat', 'lon'), parts along dimension 0, may hold values from -230 to 230
- w_in: bfloat16 [128, 8], replicated, may hold values from -2 to 2
- w_dw: bfloat16 [2, 128, 9], replicated, may hold values from -2 to 2
- w_pw: bfloat16 [2, 128, 128], replicated, may hold values from -0.5 to 0.5
- b_pw: float32 [2, 128], replicated, may hold values from -3 to 3
- w_out: bfloat16 [8, 128], replicated, may hold values from -0.5 to 0.5
Outputs:
- next_state: float32 [16, 32, 256], P('members', 'lat', 'lon'), parts along dimension 0
- frames: float32 [64, 8, 32, 256], P('members', None, 'lat', 'lon'), parts along dimension 0
- stretch: float32 [64], P('members'), parts along dimension 0
The draws below stay inside these ranges and needn't reach their ends.
There are 2 independent parts, one for each index of `members`. The reference program is written for one: setup_inputs(seed, part) draws one part's arguments, and reference() takes and returns one part's arrays. A program takes and returns all parts, laid end to end along the dimension named above; an argument that names none is the same for every part. Nothing has to cross between parts.
All inputs are finite; a program needn't handle non-finite values.
Results may differ from the reference program's by a relative error of at most 0.011.
Values may be sent and summed in bfloat16 or wider, within the bound.
A program may use at most 128 MiB of HBM per device.

```python
import math
import jax
import jax.numpy as jnp
from jax import lax

VARS = 8
CH = 128
DIRS = 32
LAYERS = 2
NLAT = 32
NLON = 256


def draw_tangents(key, part):
    key_base, key_column, key_row, key_shared = jax.random.split(key, 4)
    full_shape = (DIRS, VARS, NLAT, NLON)
    noise_field = jnp.clip(jax.random.normal(key_base, full_shape, jnp.float32), -4.0, 4.0)
    shared = jnp.clip(jax.random.normal(key_shared, (1, VARS, NLAT, NLON), jnp.float32), -4.0, 4.0)
    weighting = 0.4
    blended = noise_field + 0.5 * jnp.roll(noise_field, 1, axis=0) + weighting * shared
    column = jnp.exp(jax.random.uniform(key_column, (DIRS, 1, 1, 1), jnp.float32, math.log(0.3), math.log(3.0)))
    growth = (1.0 + 2.0 * jnp.arange(NLAT, dtype=jnp.float32) / NLAT) / 3.0
    jitter = jnp.exp(jax.random.uniform(key_row, (NLAT,), jnp.float32, 0.0, math.log(10.0)))
    return blended * column * (growth * jitter)[None, None, :, None]


def steps_of(key, dims, pieces, low, high):
    loudness, own = 1.0, jax.random.fold_in(key, 6)
    for dim, parts in pieces:
        steps = jnp.exp(jax.random.uniform(jax.random.fold_in(own, dim), (parts,), jnp.float32, low / len(pieces), high / len(pieces)))
        loudness = loudness * jnp.repeat(steps, dims[dim] // parts).reshape([-1 if axis == dim else 1 for axis in range(len(dims))])
    return loudness


def bell_draw(rng, shape, spread, limit, cuts=(), held_as=jnp.bfloat16):
    result = jax.random.normal(rng, shape, jnp.float32) * spread
    if len(cuts) > 0:
        result = steps_of(rng, shape, cuts, -0.22, 0.18) * result
    return jnp.clip(result, min=-limit, max=limit).astype(held_as)


def setup_inputs(seed: int = 0, part: int = 0) -> dict:
    key_of = jax.random.split(jax.random.key(seed), 8)
    own_keys = jax.random.split(jax.random.fold_in(key_of[7], part), 8)
    state = bell_draw(own_keys[0], (VARS, NLAT, NLON), 1.0, 6.0, ((1, 8), (2, 2)), jnp.float32)
    tangents = draw_tangents(jax.random.fold_in(jax.random.fold_in(key_of[7], part), 71), part)
    w_in = bell_draw(key_of[2], (CH, VARS), VARS ** -0.5, 2.0)
    w_dw = bell_draw(key_of[3], (LAYERS, CH, 9), 0.35, 2.0)
    w_pw = bell_draw(key_of[4], (LAYERS, CH, CH), CH ** -0.5, 0.5)
    b_pw = bell_draw(key_of[5], (LAYERS, CH), 0.5, 3.0, (), jnp.float32)
    w_out = bell_draw(key_of[6], (VARS, CH), CH ** -0.5, 0.5)
    return dict(state=state, tangents=tangents, w_in=w_in, w_dw=w_dw, w_pw=w_pw, b_pw=b_pw, w_out=w_out)


def spread_taps(padded, kernel, height, breadth):
    total = jnp.zeros(padded.shape[:2] + (height, breadth), jnp.float32)
    for row_shift in range(3):
        for col_shift in range(3):
            window = padded[:, :, row_shift:row_shift + height, col_shift:col_shift + breadth]
            total = total + kernel[:, 3 * row_shift + col_shift][None, :, None, None] * window.astype(jnp.float32)
    return total

def depthwise(field, kernel):
    padded = jnp.pad(field, ((0, 0), (1, 1), (0, 0)))
    padded = jnp.concatenate([padded[:, :, -1:], padded, padded[:, :, :1]], axis=2)
    return spread_taps(padded[None], kernel, NLAT, NLON)[0]

def reference(state, tangents, w_in, w_dw, w_pw, b_pw, w_out):
    kernels = w_dw.astype(jnp.float32)
    hidden = jnp.dot(w_in.astype(jnp.float32), state.astype(jnp.bfloat16).reshape(VARS, -1).astype(jnp.float32), preferred_element_type=jnp.float32).astype(jnp.bfloat16)
    slopes = []
    for layer_index in range(LAYERS):
        mixed = depthwise(hidden.reshape(CH, NLAT, NLON), kernels[layer_index]).reshape(CH, -1).astype(jnp.bfloat16)
        linear = jnp.dot(w_pw[layer_index].astype(jnp.float32), mixed.astype(jnp.float32), preferred_element_type=jnp.float32) + b_pw[layer_index][:, None]
        squashed = jnp.tanh(linear)
        slopes.append(1.0 - squashed * squashed)
        hidden = (hidden.astype(jnp.float32) + squashed).astype(jnp.bfloat16)
    next_state = state + jnp.dot(w_out.astype(jnp.float32), hidden.astype(jnp.float32), preferred_element_type=jnp.float32).reshape(VARS, NLAT, NLON)

    def push_one(direction):
        moving = jnp.dot(w_in.astype(jnp.float32), direction.astype(jnp.bfloat16).reshape(VARS, -1).astype(jnp.float32), preferred_element_type=jnp.float32).astype(jnp.bfloat16)
        for layer_index in range(LAYERS):
            mixed = depthwise(moving.reshape(CH, NLAT, NLON), kernels[layer_index]).reshape(CH, -1).astype(jnp.bfloat16)
            linear = jnp.dot(w_pw[layer_index].astype(jnp.float32), mixed.astype(jnp.float32), preferred_element_type=jnp.float32)
            moving = (moving.astype(jnp.float32) + slopes[layer_index] * linear).astype(jnp.bfloat16)
        return direction + jnp.dot(w_out.astype(jnp.float32), moving.astype(jnp.float32), preferred_element_type=jnp.float32).reshape(VARS, NLAT, NLON)
    pushed = lax.map(push_one, tangents).reshape(DIRS, -1)
    gram = jnp.dot(pushed.astype(jnp.float32), pushed.T.astype(jnp.float32), precision=lax.Precision.HIGHEST, preferred_element_type=jnp.float32)
    lower = jnp.linalg.cholesky(gram)
    measure = float(VARS * NLAT * NLON)
    solved = lax.linalg.triangular_solve(lower, pushed, left_side=True, lower=True)
    frames = (solved * jnp.sqrt(jnp.float32(measure))).reshape(DIRS, VARS, NLAT, NLON)
    stretch = jnp.log(jnp.diagonal(lower)) - 0.5 * jnp.log(jnp.float32(measure))
    return (next_state, frames, stretch)
```

```python
import functools
import math

import jax
import jax.numpy as jnp
from jax import lax
from jax.experimental import pallas as pl
from jax.experimental.pallas import tpu as pltpu
from jax.sharding import PartitionSpec as P

F32 = jnp.float32
BF16 = jnp.bfloat16
BLOCK = 4
HIGH = lax.Precision.HIGHEST


def dot(a, b, ca, cb, precision=None):
    return lax.dot_general(
        a, b, (((ca,), (cb,)), ((), ())), precision=precision, preferred_element_type=F32
    )


def moved(tile, src, dst):
    shift = (dst - src) % 128
    return pltpu.roll(tile, shift, 1) if shift else tile


def kernel(
    lats,
    lons,
    st_ref, tg_ref, win_ref, dw_ref, pw_ref, b_ref, wout_ref,
    ns_ref, fr_ref, sr_ref,
    send_n, send_s, recv_n, recv_s, eo, eh, eof, ehf,
    w0, w1, wf, kt, slope0, slope1, t1, c0, c2, mixb, tan2, halo, push, gbuf,
    ssem, rsem, gssem, grsem,
):
    lat = lax.axis_index("lat")
    lon = lax.axis_index("lon")
    other = 1 - lon
    n = lats * lons
    me = lat * lons + lon
    has_n = lat > 0
    has_s = lat < lats - 1

    barrier = pltpu.get_barrier_semaphore()

    @pl.loop(1, n)
    def _(i):
        q = lax.rem(me + i, n)
        pl.semaphore_signal(
            barrier, inc=1,
            device_id={"lat": q // lons, "lon": lax.rem(q, lons)},
            device_id_type=pl.DeviceIdType.MESH,
        )

    lane = lax.broadcasted_iota(jnp.int32, (32, 128), 1)

    def own_rows(ref, base):
        return [ref[pl.ds(base + r, 8, stride=4), :] for r in range(4)]

    def prep(d, edge):
        r = own_rows(tg_ref, d * 32)
        o = pl.multiple_of(d * 16, 16)
        send_n[pl.ds(o, 16), :] = jnp.concatenate(r[:2], axis=0).astype(BF16)
        send_s[pl.ds(o, 16), :] = jnp.concatenate(r[2:], axis=0).astype(BF16)
        x = jnp.concatenate(r, axis=0)
        for c, col in enumerate((0, 1, 126, 127)):
            rolled = pltpu.roll(x, lax.rem(c * 32 - col + 128 + d, 128), 1)
            edge = jnp.where(lane == c * 32 + d, rolled, edge)
        return edge

    edge = lax.fori_loop(0, 32, prep, jnp.zeros((32, 128), F32))
    r = own_rows(st_ref, 0)
    send_n[512:528, :] = jnp.concatenate(r[:2], axis=0).astype(BF16)
    send_s[512:528, :] = jnp.concatenate(r[2:], axis=0).astype(BF16)
    x = jnp.concatenate(r, axis=0)
    edge2 = jnp.zeros((32, 128), F32)
    for c, col in enumerate((0, 1, 126, 127)):
        edge2 = jnp.where(lane == c, moved(x, col, c), edge2)
    eo[16:48, 0:128] = edge.astype(BF16)
    eo[16:48, 128:256] = edge2.astype(BF16)

    pl.semaphore_wait(barrier, n - 1)

    def remote(i, src, dst, dlat, dlon):
        return pltpu.make_async_remote_copy(
            src_ref=src, dst_ref=dst, send_sem=ssem.at[i], recv_sem=rsem.at[i],
            device_id={"lat": dlat, "lon": dlon},
            device_id_type=pl.DeviceIdType.MESH,
        )

    across = remote(0, eo.at[pl.ds(16, 32)], eh.at[pl.ds(16, 32)], lat, other)
    north = [
        remote(1, eo.at[pl.ds(16, 16)], eh.at[pl.ds(48, 16)], lat - 1, other),
        remote(2, eo.at[pl.ds(16, 16)], eo.at[pl.ds(48, 16)], lat - 1, lon),
        remote(3, send_n, recv_s, lat - 1, lon),
    ]
    south = [
        remote(4, eo.at[pl.ds(32, 16)], eh.at[pl.ds(0, 16)], lat + 1, other),
        remote(5, eo.at[pl.ds(32, 16)], eo.at[pl.ds(0, 16)], lat + 1, lon),
        remote(6, send_s, recv_n, lat + 1, lon),
    ]
    across.start()

    @pl.when(has_n)
    def _():
        for c in north:
            c.start()

    @pl.when(has_s)
    def _():
        for c in south:
            c.start()

    @pl.when(jnp.logical_not(has_n))
    def _():
        recv_n[...] = jnp.zeros_like(recv_n)
        eo[0:16, :] = jnp.zeros((16, 256), BF16)
        eh[0:16, :] = jnp.zeros((16, 256), BF16)

    @pl.when(jnp.logical_not(has_s))
    def _():
        recv_s[...] = jnp.zeros_like(recv_s)
        eo[48:64, :] = jnp.zeros((16, 256), BF16)
        eh[48:64, :] = jnp.zeros((16, 256), BF16)

    eye = (
        lax.broadcasted_iota(jnp.int32, (128, 128), 0)
        == lax.broadcasted_iota(jnp.int32, (128, 128), 1)
    ).astype(BF16)
    win_t = dot(win_ref[...], eye, 0, 0)
    k0 = dot(dw_ref[0], eye, 0, 0)
    kt[0:9, :] = dot(dw_ref[1], eye, 0, 0)
    taps = jnp.concatenate([win_t * k0[t : t + 1, :] for t in range(9)], axis=0)
    comp = dot(taps, pw_ref[0].astype(F32), 1, 1, HIGH)
    wf[...] = jnp.zeros_like(wf)
    for out in range(6):
        cols = slice(out * 128, out * 128 + 128)
        wf[(out + 1) * 8 : (out + 2) * 8, cols] = win_t
    w0[...] = wf[0:64, :].astype(BF16)
    wf[0:64, :] = jnp.zeros((64, 768), F32)
    for out in range(6):
        cols = slice(out * 128, out * 128 + 128)
        for a in range(3):
            for s in range(3):
                base = s * 64 + (out + a) * 8
                t = 3 * a + s
                wf[base : base + 8, cols] = comp[t * 8 : t * 8 + 8, :]
    w1[...] = wf[...].astype(BF16)

    across.wait()

    @pl.when(has_n)
    def _():
        for c in north:
            c.wait_send()
        for c in south:
            c.wait_recv()

    @pl.when(has_s)
    def _():
        for c in south:
            c.wait_send()
        for c in north:
            c.wait_recv()

    eof[...] = eo[...].astype(F32)
    ehf[...] = eh[...].astype(F32)

    lane64 = lax.broadcasted_iota(jnp.int32, (64, 128), 1)
    own, oth = eof[:, 0:128], ehf[:, 0:128]
    own2, oth2 = eof[:, 128:256], ehf[:, 128:256]
    parts = (
        ((oth, 64), (own, 96), (oth2, 2), (own2, 3)),
        ((oth, 96), (oth, 0), (oth2, 3), (oth2, 0)),
        ((own, 0), (oth, 32), (own2, 0), (oth2, 1)),
    )
    rim = []
    for a, b, c, d in parts:
        v = moved(d[0], d[1], 65)
        v = jnp.where(lane64 < 65, moved(c[0], c[1], 64), v)
        v = jnp.where(lane64 < 64, moved(b[0], b[1], 32), v)
        v = jnp.where(lane64 < 32, moved(a[0], a[1], 0), v)
        rim.append(jnp.where(lane64 < 66, v, 0.0))

    def shifted(x, left, right):
        l = jnp.where(lane64 == 0, left, pltpu.roll(x, 1, 1))
        r = jnp.where(lane64 == 127, right, pltpu.roll(x, 127, 1))
        return jnp.concatenate([l, x, r], axis=0)

    def field(ref, base, o):
        return jnp.concatenate(
            [recv_n[pl.ds(o, 16), :].astype(F32)]
            + own_rows(ref, base)
            + [recv_s[pl.ds(o, 16), :].astype(F32)],
            axis=0,
        )

    bias0 = jnp.concatenate([b_ref[0:1, :]] * 6, axis=1)
    col = lax.broadcasted_iota(jnp.int32, (1, 768), 1)
    keep = jnp.logical_and(
        jnp.logical_or(has_n, col >= 128), jnp.logical_or(has_s, col < 640)
    ).astype(F32)

    x3 = jnp.concatenate([jnp.concatenate(rim, axis=0),
                          shifted(field(st_ref, 0, 512),
                                  moved(oth2, 3, 0), moved(oth2, 0, 127))], axis=1)
    x3 = x3.astype(BF16)
    base = dot(x3[64:128], w0[...], 0, 0)
    lin = dot(x3, w1[...], 0, 0)
    squash = jnp.tanh(lin[128:256] + bias0) * keep
    slope0[...] = keep - squash * squash
    t1[0:128, :] = base[128:256] + squash
    edge_sq = jnp.tanh(lin[64:72] + bias0) * keep
    edge_slope = keep - edge_sq * edge_sq
    edge_act = base[64:72] + edge_sq
    left = base[0:32] + edge_slope[0:1] * lin[0:32]
    right = base[32:64] + edge_slope[1:2] * lin[32:64]
    for r in range(4):
        for side, (b, dirs, act) in enumerate(
            ((0, left, edge_act[0:1]), (2, right, edge_act[1:2]))
        ):
            def tapped(u):
                return sum(
                    kt[3 * a + b : 3 * a + b + 1, :] * u[:, (r + a) * 128 : (r + a) * 128 + 128]
                    for a in range(3)
                )
            i = r * 2 + side
            halo[i, 0:32, :] = tapped(dirs)
            halo[i, 32:33, :] = tapped(act)

    def conv(row0, d, j, slot):
        for r in range(4):
            u = [t1[row0 : row0 + 128, (r + a) * 128 : (r + a) * 128 + 128] for a in range(3)]
            tap = lambda b: sum(kt[3 * a + b : 3 * a + b + 1, :] * u[a] for a in range(3))
            c0[r, 8:136, :] = tap(0)
            c0[r, 7:8, :] = halo[r * 2, pl.ds(d, 1), :]
            c2[r, 0:128, :] = tap(2)
            c2[r, 128:129, :] = halo[r * 2 + 1, pl.ds(d, 1), :]
            mix = tap(1) + c0[r, 7:135, :] + c2[r, 1:129, :]
            o = (slot * 4 + r) * 128
            mixb[o : o + 128, :] = mix.astype(BF16)

    conv(0, 32, 0, 0)
    lin = dot(mixb[0:512, :], pw_ref[1], 1, 1)
    for r in range(4):
        squash = jnp.tanh(lin[r * 128 : r * 128 + 128] + b_ref[1:2, :])
        slope1[r * 128 : r * 128 + 128, :] = 1.0 - squash * squash
        act = t1[0:128, (r + 1) * 128 : (r + 2) * 128] + squash
        tan2[r * 128 : r * 128 + 128, :] = act.astype(BF16)
    out = dot(wout_ref[...], tan2[0:512, :], 1, 1)
    for r in range(4):
        rows = pl.ds(r, 8, stride=4)
        ns_ref[rows, :] = st_ref[rows, :] + out[:, r * 128 : r * 128 + 128]

    @pl.loop(0, 32 // BLOCK)
    def _(blk):
        pieces = []
        for j in range(BLOCK):
            d = blk * BLOCK + j
            x = field(tg_ref, d * 32, pl.multiple_of(d * 16, 16))
            pieces.append(
                shifted(
                    x,
                    pltpu.roll(ehf[:, 0:128], 32 - d, 1),
                    pltpu.roll(ehf[:, 0:128], 127 - d, 1),
                )
            )
        x3 = jnp.concatenate(pieces, axis=1).astype(BF16)
        base = dot(x3[64:128], w0[...], 0, 0)
        lin = dot(x3, w1[...], 0, 0)
        for j in range(BLOCK):
            rows = slice(j * 128, j * 128 + 128)
            t1[rows, :] = base[rows] + slope0[...] * lin[rows]
        for j in range(BLOCK):
            conv(j * 128, blk * BLOCK + j, j, j)
        lin = dot(mixb[...], pw_ref[1], 1, 1)
        for j in range(BLOCK):
            for r in range(4):
                o = (j * 4 + r) * 128
                v = t1[j * 128 : j * 128 + 128, (r + 1) * 128 : (r + 2) * 128]
                v = v + slope1[r * 128 : r * 128 + 128, :] * lin[o : o + 128]
                tan2[o : o + 128, :] = v.astype(BF16)
        out = dot(wout_ref[...], tan2[...], 1, 1)
        for j in range(BLOCK):
            d = blk * BLOCK + j
            for r in range(4):
                o = (j * 4 + r) * 128
                push[r, pl.ds(d, 8, stride=32), :] = (
                    tg_ref[pl.ds(d * 32 + r, 8, stride=4), :] + out[:, o : o + 128]
                )

    gram = jnp.zeros((32, 32), F32)
    for v in range(8):
        for r in range(4):
            p = push[r, v * 32 : v * 32 + 32, :]
            gram = gram + dot(p, p, 1, 1, HIGH)
    gbuf[me] = jnp.concatenate([gram[i * 8 : i * 8 + 8] for i in range(4)], axis=1)

    def gram_copy(i):
        q = lax.rem(me + i, n)
        return pltpu.make_async_remote_copy(
            src_ref=gbuf.at[me], dst_ref=gbuf.at[me],
            send_sem=gssem.at[i], recv_sem=grsem.at[i],
            device_id={"lat": q // lons, "lon": lax.rem(q, lons)},
            device_id_type=pl.DeviceIdType.MESH,
        )

    @pl.loop(1, n)
    def _(i):
        gram_copy(i).start()

    @pl.loop(1, n)
    def _(i):
        gram_copy(i).wait()

    total = lax.fori_loop(1, n, lambda i, g: g + gbuf[i], gbuf[0])
    g = jnp.concatenate([total[:, i * 32 : i * 32 + 32] for i in range(4)], axis=0)
    sub = lax.broadcasted_iota(jnp.int32, (32, 32), 0)
    lan = lax.broadcasted_iota(jnp.int32, (32, 32), 1)
    unit = sub == lan
    a = jnp.concatenate([g, unit.astype(F32)], axis=1)
    row_id = lax.broadcasted_iota(jnp.int32, (32, 1), 0)
    for k in range(32):
        row = a[k : k + 1, :]
        factor = jnp.where(row_id > k, a[:, k : k + 1], 0.0)
        a = a - factor * (row / a[k : k + 1, k : k + 1])
    measure = float(1024 * 4 * n)
    left = jnp.where(unit, a[:, 0:32], 0.0)
    dcol = jnp.sum(left, axis=1, keepdims=True)
    drow = jnp.sum(left, axis=0, keepdims=True)
    inv = a[:, 32:64] * (math.sqrt(measure) / jnp.sqrt(dcol))
    sr_ref[...] = 0.5 * jnp.log(drow) - 0.5 * math.log(measure)
    for v in range(8):
        for r in range(4):
            fr_ref[pl.ds(v * 4 + r, 32, stride=32), :] = dot(
                inv, push[r, v * 32 : v * 32 + 32, :], 1, 0, HIGH
            )


def per_device(lats, lons, state, tangents, w_in, w_dw, w_pw, b_pw, w_out):
    n = lats * lons
    vm = pl.BlockSpec(memory_space=pltpu.VMEM)
    stepped, frames, stretch = pl.pallas_call(
        functools.partial(kernel, lats, lons),
        out_shape=(
            jax.ShapeDtypeStruct((32, 128), F32),
            jax.ShapeDtypeStruct((1024, 128), F32),
            jax.ShapeDtypeStruct((1, 32), F32),
        ),
        in_specs=[vm] * 7,
        out_specs=(vm,) * 3,
        scratch_shapes=[
            pltpu.VMEM((528, 128), BF16), pltpu.VMEM((528, 128), BF16),
            pltpu.VMEM((528, 128), BF16), pltpu.VMEM((528, 128), BF16),
            pltpu.VMEM((64, 256), BF16), pltpu.VMEM((64, 256), BF16),
            pltpu.VMEM((64, 256), F32), pltpu.VMEM((64, 256), F32),
            pltpu.VMEM((64, 768), BF16), pltpu.VMEM((192, 768), BF16),
            pltpu.VMEM((192, 768), F32), pltpu.VMEM((16, 128), F32),
            pltpu.VMEM((128, 768), F32), pltpu.VMEM((512, 128), F32),
            pltpu.VMEM((BLOCK * 128, 768), F32),
            pltpu.VMEM((4, 136, 128), F32), pltpu.VMEM((4, 136, 128), F32),
            pltpu.VMEM((BLOCK * 512, 128), BF16), pltpu.VMEM((BLOCK * 512, 128), BF16),
            pltpu.VMEM((8, 40, 128), F32), pltpu.VMEM((4, 256, 128), F32),
            pltpu.VMEM((n, 8, 128), F32),
            pltpu.SemaphoreType.DMA((7,)), pltpu.SemaphoreType.DMA((7,)),
            pltpu.SemaphoreType.DMA((n,)), pltpu.SemaphoreType.DMA((n,)),
        ],
        compiler_params=pltpu.CompilerParams(
            collective_id=0, has_side_effects=True, vmem_limit_bytes=48 * 1024 * 1024
        ),
    )(
        state.reshape(32, 128), tangents.reshape(1024, 128),
        w_in, w_dw, w_pw, b_pw, w_out,
    )
    return stepped.reshape(state.shape), frames.reshape(tangents.shape), stretch.reshape(32)


def solution(mesh):
    placed = (P("members", "lat", "lon"), P("members", None, "lat", "lon"), P(), P(), P(), P(), P())
    return jax.shard_map(
        functools.partial(per_device, mesh.shape["lat"], mesh.shape["lon"]),
        mesh=mesh,
        in_specs=placed,
        out_specs=(P("members", "lat", "lon"), P("members", None, "lat", "lon"), P("members")),
        check_vma=False,
    )
```

```python
import functools
import math

import jax
import jax.numpy as jnp
from jax import lax
from jax.experimental import pallas as pl
from jax.experimental.pallas import tpu as pltpu
from jax.sharding import PartitionSpec as P

F32 = jnp.float32
BF16 = jnp.bfloat16
BLOCK = 4
HIGH = lax.Precision.HIGHEST


def dot(a, b, ca, cb, precision=None):
    return lax.dot_general(
        a, b, (((ca,), (cb,)), ((), ())), precision=precision, preferred_element_type=F32
    )


def moved(tile, src, dst):
    shift = (dst - src) % 128
    return pltpu.roll(tile, shift, 1) if shift else tile


def kernel(
    lats,
    lons,
    st_ref, tg_ref, win_ref, dw_ref, pw_ref, b_ref, wout_ref,
    ns_ref, fr_ref, sr_ref,
    send_n, send_s, recv_n, recv_s, eo, eh, eof, ehf,
    w0, w1, wf, kt, slope0, slope1, t1, c0, c2, mixb, tan2, halo, push, gbuf, pair,
    ssem, rsem, gssem, grsem,
):
    lat = lax.axis_index("lat")
    lon = lax.axis_index("lon")
    other = 1 - lon
    n = lats * lons
    me = lat * lons + lon
    has_n = lat > 0
    has_s = lat < lats - 1

    barrier = pltpu.get_barrier_semaphore()

    @pl.loop(1, n)
    def _(i):
        q = lax.rem(me + i, n)
        pl.semaphore_signal(
            barrier, inc=1,
            device_id={"lat": q // lons, "lon": lax.rem(q, lons)},
            device_id_type=pl.DeviceIdType.MESH,
        )

    lane = lax.broadcasted_iota(jnp.int32, (32, 128), 1)

    def own_rows(ref, base):
        return [ref[pl.ds(base + r, 8, stride=4), :] for r in range(4)]

    def prep(d, edge):
        r = own_rows(tg_ref, d * 32)
        o = pl.multiple_of(d * 16, 16)
        send_n[pl.ds(o, 16), :] = jnp.concatenate(r[:2], axis=0).astype(BF16)
        send_s[pl.ds(o, 16), :] = jnp.concatenate(r[2:], axis=0).astype(BF16)
        x = jnp.concatenate(r, axis=0)
        for c, col in enumerate((0, 1, 126, 127)):
            rolled = pltpu.roll(x, lax.rem(c * 32 - col + 128 + d, 128), 1)
            edge = jnp.where(lane == c * 32 + d, rolled, edge)
        return edge

    edge = lax.fori_loop(0, 32, prep, jnp.zeros((32, 128), F32))
    r = own_rows(st_ref, 0)
    send_n[512:528, :] = jnp.concatenate(r[:2], axis=0).astype(BF16)
    send_s[512:528, :] = jnp.concatenate(r[2:], axis=0).astype(BF16)
    x = jnp.concatenate(r, axis=0)
    edge2 = jnp.zeros((32, 128), F32)
    for c, col in enumerate((0, 1, 126, 127)):
        edge2 = jnp.where(lane == c, moved(x, col, c), edge2)
    eo[16:48, 0:128] = edge.astype(BF16)
    eo[16:48, 128:256] = edge2.astype(BF16)

    pl.semaphore_wait(barrier, n - 1)

    def remote(i, src, dst, dlat, dlon):
        return pltpu.make_async_remote_copy(
            src_ref=src, dst_ref=dst, send_sem=ssem.at[i], recv_sem=rsem.at[i],
            device_id={"lat": dlat, "lon": dlon},
            device_id_type=pl.DeviceIdType.MESH,
        )

    across = remote(0, eo.at[pl.ds(16, 32)], eh.at[pl.ds(16, 32)], lat, other)
    north = [
        remote(1, eo.at[pl.ds(16, 16)], eh.at[pl.ds(48, 16)], lat - 1, other),
        remote(2, eo.at[pl.ds(16, 16)], eo.at[pl.ds(48, 16)], lat - 1, lon),
        remote(3, send_n.at[pl.ds(512, 16)], recv_s.at[pl.ds(512, 16)], lat - 1, lon),
    ]
    south = [
        remote(4, eo.at[pl.ds(32, 16)], eh.at[pl.ds(0, 16)], lat + 1, other),
        remote(5, eo.at[pl.ds(32, 16)], eo.at[pl.ds(0, 16)], lat + 1, lon),
        remote(6, send_s.at[pl.ds(512, 16)], recv_n.at[pl.ds(512, 16)], lat + 1, lon),
    ]

    def piece(blk, up):
        o = pl.ds(pl.multiple_of(blk * (BLOCK * 16), BLOCK * 16), BLOCK * 16)
        src, dst = (send_n, recv_s) if up else (send_s, recv_n)
        i = 7 + 2 * blk + (0 if up else 1)
        return remote(i, src.at[o], dst.at[o], lat - 1 if up else lat + 1, lon)

    blocks = 32 // BLOCK
    across.start()

    @pl.when(has_n)
    def _():
        for c in north:
            c.start()

    @pl.when(has_s)
    def _():
        for c in south:
            c.start()

    for blk in range(blocks):

        @pl.when(has_n)
        def _():
            piece(blk, True).start()

        @pl.when(has_s)
        def _():
            piece(blk, False).start()

    @pl.when(jnp.logical_not(has_n))
    def _():
        recv_n[...] = jnp.zeros_like(recv_n)
        eo[0:16, :] = jnp.zeros((16, 256), BF16)
        eh[0:16, :] = jnp.zeros((16, 256), BF16)

    @pl.when(jnp.logical_not(has_s))
    def _():
        recv_s[...] = jnp.zeros_like(recv_s)
        eo[48:64, :] = jnp.zeros((16, 256), BF16)
        eh[48:64, :] = jnp.zeros((16, 256), BF16)

    win_t = win_ref[...].astype(F32)
    k0 = [dw_ref[t, 0:1, :].astype(F32) for t in range(9)]
    for t in range(9):
        kt[t : t + 1, :] = dw_ref[t, 1:2, :].astype(F32)
    taps = jnp.concatenate([win_t * k0[t] for t in range(9)], axis=0)
    comp = dot(taps, pw_ref[0].astype(F32), 1, 1, HIGH)
    wf[...] = jnp.zeros_like(wf)
    for out in range(6):
        cols = slice(out * 128, out * 128 + 128)
        wf[(out + 1) * 8 : (out + 2) * 8, cols] = win_t
    w0[...] = wf[0:64, :].astype(BF16)
    wf[0:64, :] = jnp.zeros((64, 768), F32)
    for out in range(6):
        cols = slice(out * 128, out * 128 + 128)
        for a in range(3):
            for s in range(3):
                base = s * 64 + (out + a) * 8
                t = 3 * a + s
                wf[base : base + 8, cols] = comp[t * 8 : t * 8 + 8, :]
    w1[...] = wf[...].astype(BF16)

    across.wait()

    @pl.when(has_n)
    def _():
        for c in north:
            c.wait_send()
        for c in south:
            c.wait_recv()

    @pl.when(has_s)
    def _():
        for c in south:
            c.wait_send()
        for c in north:
            c.wait_recv()

    eof[...] = eo[...].astype(F32)
    ehf[...] = eh[...].astype(F32)

    lane64 = lax.broadcasted_iota(jnp.int32, (64, 128), 1)
    own, oth = eof[:, 0:128], ehf[:, 0:128]
    own2, oth2 = eof[:, 128:256], ehf[:, 128:256]
    parts = (
        ((oth, 64), (own, 96), (oth2, 2), (own2, 3)),
        ((oth, 96), (oth, 0), (oth2, 3), (oth2, 0)),
        ((own, 0), (oth, 32), (own2, 0), (oth2, 1)),
    )
    rim = []
    for a, b, c, d in parts:
        v = moved(d[0], d[1], 65)
        v = jnp.where(lane64 < 65, moved(c[0], c[1], 64), v)
        v = jnp.where(lane64 < 64, moved(b[0], b[1], 32), v)
        v = jnp.where(lane64 < 32, moved(a[0], a[1], 0), v)
        rim.append(jnp.where(lane64 < 66, v, 0.0))

    def shifted(x, left, right):
        l = jnp.where(lane64 == 0, left, pltpu.roll(x, 1, 1))
        r = jnp.where(lane64 == 127, right, pltpu.roll(x, 127, 1))
        return jnp.concatenate([l, x, r], axis=0)

    def field(ref, base, o):
        return jnp.concatenate(
            [recv_n[pl.ds(o, 16), :].astype(F32)]
            + own_rows(ref, base)
            + [recv_s[pl.ds(o, 16), :].astype(F32)],
            axis=0,
        )

    bias0 = jnp.concatenate([b_ref[0:1, :]] * 6, axis=1)
    col = lax.broadcasted_iota(jnp.int32, (1, 768), 1)
    keep = jnp.logical_and(
        jnp.logical_or(has_n, col >= 128), jnp.logical_or(has_s, col < 640)
    ).astype(F32)

    x3 = jnp.concatenate([jnp.concatenate(rim, axis=0),
                          shifted(field(st_ref, 0, 512),
                                  moved(oth2, 3, 0), moved(oth2, 0, 127))], axis=1)
    x3 = x3.astype(BF16)
    base = dot(x3[64:128], w0[...], 0, 0)
    lin = dot(x3, w1[...], 0, 0)
    squash = jnp.tanh(lin[128:256] + bias0) * keep
    slope0[...] = keep - squash * squash
    t1[0:128, :] = base[128:256] + squash
    edge_sq = jnp.tanh(lin[64:72] + bias0) * keep
    edge_slope = keep - edge_sq * edge_sq
    edge_act = base[64:72] + edge_sq
    left = base[0:32] + edge_slope[0:1] * lin[0:32]
    right = base[32:64] + edge_slope[1:2] * lin[32:64]
    for r in range(4):
        for side, (b, dirs, act) in enumerate(
            ((0, left, edge_act[0:1]), (2, right, edge_act[1:2]))
        ):
            def tapped(u):
                return sum(
                    kt[3 * a + b : 3 * a + b + 1, :] * u[:, (r + a) * 128 : (r + a) * 128 + 128]
                    for a in range(3)
                )
            i = r * 2 + side
            halo[i, 0:32, :] = tapped(dirs)
            halo[i, 32:33, :] = tapped(act)

    def conv(row0, d, j, slot):
        for r in range(4):
            u = [t1[row0 : row0 + 128, (r + a) * 128 : (r + a) * 128 + 128] for a in range(3)]
            tap = lambda b: sum(kt[3 * a + b : 3 * a + b + 1, :] * u[a] for a in range(3))
            c0[r, 8:136, :] = tap(0)
            c0[r, 7:8, :] = halo[r * 2, pl.ds(d, 1), :]
            c2[r, 0:128, :] = tap(2)
            c2[r, 128:129, :] = halo[r * 2 + 1, pl.ds(d, 1), :]
            mix = tap(1) + c0[r, 7:135, :] + c2[r, 1:129, :]
            o = (slot * 4 + r) * 128
            mixb[o : o + 128, :] = mix.astype(BF16)

    conv(0, 32, 0, 0)
    lin = dot(mixb[0:512, :], pw_ref[1], 1, 1)
    for r in range(4):
        squash = jnp.tanh(lin[r * 128 : r * 128 + 128] + b_ref[1:2, :])
        slope1[r * 128 : r * 128 + 128, :] = 1.0 - squash * squash
        act = t1[0:128, (r + 1) * 128 : (r + 2) * 128] + squash
        tan2[r * 128 : r * 128 + 128, :] = act.astype(BF16)
    out = dot(wout_ref[...], tan2[0:512, :], 1, 1)
    for r in range(4):
        rows = pl.ds(r, 8, stride=4)
        ns_ref[rows, :] = st_ref[rows, :] + out[:, r * 128 : r * 128 + 128]

    @pl.loop(0, blocks)
    def _(blk):
        @pl.when(has_n)
        def _():
            piece(blk, True).wait_send()
            piece(blk, False).wait_recv()

        @pl.when(has_s)
        def _():
            piece(blk, False).wait_send()
            piece(blk, True).wait_recv()

        pieces = []
        for j in range(BLOCK):
            d = blk * BLOCK + j
            x = field(tg_ref, d * 32, pl.multiple_of(d * 16, 16))
            pieces.append(
                shifted(
                    x,
                    pltpu.roll(ehf[:, 0:128], 32 - d, 1),
                    pltpu.roll(ehf[:, 0:128], 127 - d, 1),
                )
            )
        x3 = jnp.concatenate(pieces, axis=1).astype(BF16)
        base = dot(x3[64:128], w0[...], 0, 0)
        lin = dot(x3, w1[...], 0, 0)
        for j in range(BLOCK):
            rows = slice(j * 128, j * 128 + 128)
            t1[rows, :] = base[rows] + slope0[...] * lin[rows]
        for j in range(BLOCK):
            conv(j * 128, blk * BLOCK + j, j, j)
        lin = dot(mixb[...], pw_ref[1], 1, 1)
        for j in range(BLOCK):
            for r in range(4):
                o = (j * 4 + r) * 128
                v = t1[j * 128 : j * 128 + 128, (r + 1) * 128 : (r + 2) * 128]
                v = v + slope1[r * 128 : r * 128 + 128, :] * lin[o : o + 128]
                tan2[o : o + 128, :] = v.astype(BF16)
        out = dot(wout_ref[...], tan2[...], 1, 1)
        for j in range(BLOCK):
            d = blk * BLOCK + j
            for r in range(4):
                o = (j * 4 + r) * 128
                push[r, pl.ds(d, 8, stride=32), :] = (
                    tg_ref[pl.ds(d * 32 + r, 8, stride=4), :] + out[:, o : o + 128]
                )

    for v in range(8):
        for r in range(4):
            p = push[r, v * 32 : v * 32 + 32, :]
            hi = p.astype(BF16)
            lo = (p - hi.astype(F32)).astype(BF16)
            o = (v * 4 + r) * 128
            pair[:, o : o + 128] = jnp.concatenate([hi, lo], axis=0)
    four = dot(pair[...], pair[...], 1, 1)
    gram = four[0:32, 0:32] + four[0:32, 32:64] + (four[32:64, 0:32] + four[32:64, 32:64])
    gbuf[me] = jnp.concatenate([gram[i * 8 : i * 8 + 8] for i in range(4)], axis=1)

    def gram_copy(i):
        q = lax.rem(me + i, n)
        return pltpu.make_async_remote_copy(
            src_ref=gbuf.at[me], dst_ref=gbuf.at[me],
            send_sem=gssem.at[i], recv_sem=grsem.at[i],
            device_id={"lat": q // lons, "lon": lax.rem(q, lons)},
            device_id_type=pl.DeviceIdType.MESH,
        )

    @pl.loop(1, n)
    def _(i):
        gram_copy(i).start()

    @pl.loop(1, n)
    def _(i):
        gram_copy(i).wait()

    total = lax.fori_loop(1, n, lambda i, g: g + gbuf[i], gbuf[0])
    g = jnp.concatenate([total[:, i * 32 : i * 32 + 32] for i in range(4)], axis=0)
    sub = lax.broadcasted_iota(jnp.int32, (32, 32), 0)
    lan = lax.broadcasted_iota(jnp.int32, (32, 32), 1)
    unit = sub == lan
    a = jnp.concatenate([g, unit.astype(F32)], axis=1)
    row_id = lax.broadcasted_iota(jnp.int32, (32, 1), 0)
    for k in range(32):
        row = a[k : k + 1, :]
        factor = jnp.where(row_id > k, a[:, k : k + 1], 0.0)
        a = a - factor * (row / a[k : k + 1, k : k + 1])
    measure = float(1024 * 4 * n)
    left = jnp.where(unit, a[:, 0:32], 0.0)
    dcol = jnp.sum(left, axis=1, keepdims=True)
    drow = jnp.sum(left, axis=0, keepdims=True)
    inv = a[:, 32:64] * (math.sqrt(measure) / jnp.sqrt(dcol))
    sr_ref[...] = 0.5 * jnp.log(drow) - 0.5 * math.log(measure)
    hi = inv.astype(BF16)
    lo = (inv - hi.astype(F32)).astype(BF16)
    both = jnp.concatenate(
        [jnp.concatenate([hi, hi], axis=1), jnp.concatenate([lo, lo], axis=1)], axis=0
    )
    for c in range(8):
        out = dot(both, pair[:, c * 512 : c * 512 + 512], 1, 0)
        out = out[0:32] + out[32:64]
        for r in range(4):
            fr_ref[pl.ds(c * 4 + r, 32, stride=32), :] = out[:, r * 128 : r * 128 + 128]


def per_device(lats, lons, state, tangents, w_in, w_dw, w_pw, b_pw, w_out):
    n = lats * lons
    vm = pl.BlockSpec(memory_space=pltpu.VMEM)
    stepped, frames, stretch = pl.pallas_call(
        functools.partial(kernel, lats, lons),
        out_shape=(
            jax.ShapeDtypeStruct((32, 128), F32),
            jax.ShapeDtypeStruct((1024, 128), F32),
            jax.ShapeDtypeStruct((1, 32), F32),
        ),
        in_specs=[vm] * 7,
        out_specs=(vm,) * 3,
        scratch_shapes=[
            pltpu.VMEM((528, 128), BF16), pltpu.VMEM((528, 128), BF16),
            pltpu.VMEM((528, 128), BF16), pltpu.VMEM((528, 128), BF16),
            pltpu.VMEM((64, 256), BF16), pltpu.VMEM((64, 256), BF16),
            pltpu.VMEM((64, 256), F32), pltpu.VMEM((64, 256), F32),
            pltpu.VMEM((64, 768), BF16), pltpu.VMEM((192, 768), BF16),
            pltpu.VMEM((192, 768), F32), pltpu.VMEM((16, 128), F32),
            pltpu.VMEM((128, 768), F32), pltpu.VMEM((512, 128), F32),
            pltpu.VMEM((BLOCK * 128, 768), F32),
            pltpu.VMEM((4, 136, 128), F32), pltpu.VMEM((4, 136, 128), F32),
            pltpu.VMEM((BLOCK * 512, 128), BF16), pltpu.VMEM((BLOCK * 512, 128), BF16),
            pltpu.VMEM((8, 40, 128), F32), pltpu.VMEM((4, 256, 128), F32),
            pltpu.VMEM((n, 8, 128), F32),
            pltpu.VMEM((64, 4096), BF16),
            pltpu.SemaphoreType.DMA((7 + 64 // BLOCK,)), pltpu.SemaphoreType.DMA((7 + 64 // BLOCK,)),
            pltpu.SemaphoreType.DMA((n,)), pltpu.SemaphoreType.DMA((n,)),
        ],
        compiler_params=pltpu.CompilerParams(
            collective_id=0, has_side_effects=True, vmem_limit_bytes=48 * 1024 * 1024
        ),
    )(
        state.reshape(32, 128), tangents.reshape(1024, 128),
        w_in.T, w_dw.transpose(2, 0, 1), w_pw, b_pw, w_out,
    )
    return stepped.reshape(state.shape), frames.reshape(tangents.shape), stretch.reshape(32)


def solution(mesh):
    placed = (P("members", "lat", "lon"), P("members", None, "lat", "lon"), P(), P(), P(), P(), P())
    return jax.shard_map(
        functools.partial(per_device, mesh.shape["lat"], mesh.shape["lon"]),
        mesh=mesh,
        in_specs=placed,
        out_specs=(P("members", "lat", "lon"), P("members", None, "lat", "lon"), P("members")),
        check_vma=False,
    )
```

```python
import functools
import math

import jax
import jax.numpy as jnp
from jax import lax
from jax.experimental import pallas as pl
from jax.experimental.pallas import tpu as pltpu
from jax.sharding import PartitionSpec as P

F32 = jnp.float32
BF16 = jnp.bfloat16
BLOCK = 8
HIGH = lax.Precision.HIGHEST


def dot(a, b, ca, cb, precision=None):
    return lax.dot_general(
        a, b, (((ca,), (cb,)), ((), ())), precision=precision, preferred_element_type=F32
    )


def each(lo, hi, body):
    if hi <= 16:
        for i in range(lo, hi):
            body(i)
    else:
        pl.loop(lo, hi)(body)


def moved(tile, src, dst):
    shift = (dst - src) % 128
    return pltpu.roll(tile, shift, 1) if shift else tile


def kernel(
    lats,
    lons,
    st_in, tg_in, win_in, dw_in, pw_in, b_in, wout_in,
    ns_ref, fr_ref, sr_ref,
    send_n, send_s, recv_n, recv_s, eo, eh, eof, ehf,
    w0, w1, wf, kt, slope0, slope1, t1, c0, c2, mixb, tan2, halo, push, gbuf, pair,
    st_ref, tg_ref, win_ref, dw_ref, pw_ref, b_ref, wout_ref,
    ssem, rsem, gssem, grsem, isem,
):
    lat = lax.axis_index("lat")
    lon = lax.axis_index("lon")
    other = 1 - lon
    n = lats * lons
    me = lat * lons + lon
    has_n = lat > 0
    has_s = lat < lats - 1

    fetch = [
        pltpu.make_async_copy(src, dst, isem.at[i])
        for i, (src, dst) in enumerate(
            (
                (tg_in, tg_ref), (st_in, st_ref), (dw_in, dw_ref), (win_in, win_ref),
                (pw_in, pw_ref), (b_in, b_ref), (wout_in, wout_ref),
            )
        )
    ]
    for c in fetch:
        c.start()
    barrier = pltpu.get_barrier_semaphore()

    def peer(i):
        q = me + i
        q = jnp.where(q >= n, q - n, q)
        return {"lat": q // lons, "lon": q % lons}

    def greet(i):
        pl.semaphore_signal(
            barrier, inc=1, device_id=peer(i), device_id_type=pl.DeviceIdType.MESH
        )

    each(1, n, greet)

    lane = lax.broadcasted_iota(jnp.int32, (32, 128), 1)
    fetch[0].wait()
    fetch[1].wait()

    def own_rows(ref, base):
        return [ref[pl.ds(base + r, 8, stride=4), :] for r in range(4)]

    def prep(d, edge):
        r = own_rows(tg_ref, d * 32)
        o = pl.multiple_of(d * 16, 16)
        send_n[pl.ds(o, 16), :] = jnp.concatenate(r[:2], axis=0).astype(BF16)
        send_s[pl.ds(o, 16), :] = jnp.concatenate(r[2:], axis=0).astype(BF16)
        x = jnp.concatenate(r, axis=0)
        for c, col in enumerate((0, 1, 126, 127)):
            rolled = pltpu.roll(x, lax.rem(c * 32 - col + 128 + d, 128), 1)
            edge = jnp.where(lane == c * 32 + d, rolled, edge)
        return edge

    edge = lax.fori_loop(0, 32, prep, jnp.zeros((32, 128), F32), unroll=8)
    r = own_rows(st_ref, 0)
    send_n[512:528, :] = jnp.concatenate(r[:2], axis=0).astype(BF16)
    send_s[512:528, :] = jnp.concatenate(r[2:], axis=0).astype(BF16)
    x = jnp.concatenate(r, axis=0)
    edge2 = jnp.zeros((32, 128), F32)
    for c, col in enumerate((0, 1, 126, 127)):
        edge2 = jnp.where(lane == c, moved(x, col, c), edge2)
    eo[16:48, 0:128] = edge.astype(BF16)
    eo[16:48, 128:256] = edge2.astype(BF16)

    pl.semaphore_wait(barrier, n - 1)

    def remote(i, src, dst, dlat, dlon):
        return pltpu.make_async_remote_copy(
            src_ref=src, dst_ref=dst, send_sem=ssem.at[i], recv_sem=rsem.at[i],
            device_id={"lat": dlat, "lon": dlon},
            device_id_type=pl.DeviceIdType.MESH,
        )

    across = remote(0, eo.at[pl.ds(16, 32)], eh.at[pl.ds(16, 32)], lat, other)
    north = [
        remote(1, eo.at[pl.ds(16, 16)], eh.at[pl.ds(48, 16)], lat - 1, other),
        remote(2, eo.at[pl.ds(16, 16)], eo.at[pl.ds(48, 16)], lat - 1, lon),
        remote(3, send_n.at[pl.ds(512, 16)], recv_s.at[pl.ds(512, 16)], lat - 1, lon),
    ]
    south = [
        remote(4, eo.at[pl.ds(32, 16)], eh.at[pl.ds(0, 16)], lat + 1, other),
        remote(5, eo.at[pl.ds(32, 16)], eo.at[pl.ds(0, 16)], lat + 1, lon),
        remote(6, send_s.at[pl.ds(512, 16)], recv_n.at[pl.ds(512, 16)], lat + 1, lon),
    ]

    def piece(blk, up):
        o = pl.ds(pl.multiple_of(blk * (BLOCK * 16), BLOCK * 16), BLOCK * 16)
        src, dst = (send_n, recv_s) if up else (send_s, recv_n)
        i = 7 + 2 * blk + (0 if up else 1)
        return remote(i, src.at[o], dst.at[o], lat - 1 if up else lat + 1, lon)

    blocks = 32 // BLOCK
    across.start()

    @pl.when(has_n)
    def _():
        for c in north:
            c.start()

    @pl.when(has_s)
    def _():
        for c in south:
            c.start()

    for blk in range(blocks):

        @pl.when(has_n)
        def _():
            piece(blk, True).start()

        @pl.when(has_s)
        def _():
            piece(blk, False).start()

    @pl.when(jnp.logical_not(has_n))
    def _():
        recv_n[...] = jnp.zeros_like(recv_n)
        eo[0:16, :] = jnp.zeros((16, 256), BF16)
        eh[0:16, :] = jnp.zeros((16, 256), BF16)

    @pl.when(jnp.logical_not(has_s))
    def _():
        recv_s[...] = jnp.zeros_like(recv_s)
        eo[48:64, :] = jnp.zeros((16, 256), BF16)
        eh[48:64, :] = jnp.zeros((16, 256), BF16)

    for c in fetch[2:]:
        c.wait()
    win_t = win_ref[...].astype(F32)
    k0 = [dw_ref[t, 0:1, :].astype(F32) for t in range(9)]
    for t in range(9):
        kt[t : t + 1, :] = dw_ref[t, 1:2, :].astype(F32)
    taps = jnp.concatenate([win_t * k0[t] for t in range(9)], axis=0)
    comp = dot(taps, pw_ref[0].astype(F32), 1, 1, HIGH)
    wf[...] = jnp.zeros_like(wf)
    for out in range(6):
        cols = slice(out * 128, out * 128 + 128)
        wf[(out + 1) * 8 : (out + 2) * 8, cols] = win_t
    w0[...] = wf[0:64, :].astype(BF16)
    wf[0:64, :] = jnp.zeros((64, 768), F32)
    for out in range(6):
        cols = slice(out * 128, out * 128 + 128)
        for a in range(3):
            for s in range(3):
                base = s * 64 + (out + a) * 8
                t = 3 * a + s
                wf[base : base + 8, cols] = comp[t * 8 : t * 8 + 8, :]
    w1[...] = wf[...].astype(BF16)

    across.wait()

    @pl.when(has_n)
    def _():
        for c in north:
            c.wait_send()
        for c in south:
            c.wait_recv()

    @pl.when(has_s)
    def _():
        for c in south:
            c.wait_send()
        for c in north:
            c.wait_recv()

    eof[...] = eo[...].astype(F32)
    ehf[...] = eh[...].astype(F32)

    lane64 = lax.broadcasted_iota(jnp.int32, (64, 128), 1)
    own, oth = eof[:, 0:128], ehf[:, 0:128]
    own2, oth2 = eof[:, 128:256], ehf[:, 128:256]
    parts = (
        ((oth, 64), (own, 96), (oth2, 2), (own2, 3)),
        ((oth, 96), (oth, 0), (oth2, 3), (oth2, 0)),
        ((own, 0), (oth, 32), (own2, 0), (oth2, 1)),
    )
    rim = []
    for a, b, c, d in parts:
        v = moved(d[0], d[1], 65)
        v = jnp.where(lane64 < 65, moved(c[0], c[1], 64), v)
        v = jnp.where(lane64 < 64, moved(b[0], b[1], 32), v)
        v = jnp.where(lane64 < 32, moved(a[0], a[1], 0), v)
        rim.append(jnp.where(lane64 < 66, v, 0.0))

    def shifted(x, left, right):
        l = jnp.where(lane64 == 0, left, pltpu.roll(x, 1, 1))
        r = jnp.where(lane64 == 127, right, pltpu.roll(x, 127, 1))
        return jnp.concatenate([l, x, r], axis=0)

    def field(ref, base, o):
        return jnp.concatenate(
            [recv_n[pl.ds(o, 16), :].astype(F32)]
            + own_rows(ref, base)
            + [recv_s[pl.ds(o, 16), :].astype(F32)],
            axis=0,
        )

    bias0 = jnp.concatenate([b_ref[0:1, :]] * 6, axis=1)
    col = lax.broadcasted_iota(jnp.int32, (1, 768), 1)
    keep = jnp.logical_and(
        jnp.logical_or(has_n, col >= 128), jnp.logical_or(has_s, col < 640)
    ).astype(F32)

    x3 = jnp.concatenate([jnp.concatenate(rim, axis=0),
                          shifted(field(st_ref, 0, 512),
                                  moved(oth2, 3, 0), moved(oth2, 0, 127))], axis=1)
    x3 = x3.astype(BF16)
    base = dot(x3[64:128], w0[...], 0, 0)
    lin = dot(x3, w1[...], 0, 0)
    squash = jnp.tanh(lin[128:256] + bias0) * keep
    slope0[...] = keep - squash * squash
    t1[0:128, :] = base[128:256] + squash
    edge_sq = jnp.tanh(lin[64:72] + bias0) * keep
    edge_slope = keep - edge_sq * edge_sq
    edge_act = base[64:72] + edge_sq
    left = base[0:32] + edge_slope[0:1] * lin[0:32]
    right = base[32:64] + edge_slope[1:2] * lin[32:64]
    for r in range(4):
        for side, (b, dirs, act) in enumerate(
            ((0, left, edge_act[0:1]), (2, right, edge_act[1:2]))
        ):
            def tapped(u):
                return sum(
                    kt[3 * a + b : 3 * a + b + 1, :] * u[:, (r + a) * 128 : (r + a) * 128 + 128]
                    for a in range(3)
                )
            i = r * 2 + side
            halo[i, 0:32, :] = tapped(dirs)
            halo[i, 32:33, :] = tapped(act)

    def conv(row0, d, j, slot):
        for r in range(4):
            u = [t1[row0 : row0 + 128, (r + a) * 128 : (r + a) * 128 + 128] for a in range(3)]
            tap = lambda b: sum(kt[3 * a + b : 3 * a + b + 1, :] * u[a] for a in range(3))
            c0[r, 8:136, :] = tap(0)
            c0[r, 7:8, :] = halo[r * 2, pl.ds(d, 1), :]
            c2[r, 0:128, :] = tap(2)
            c2[r, 128:129, :] = halo[r * 2 + 1, pl.ds(d, 1), :]
            mix = tap(1) + c0[r, 7:135, :] + c2[r, 1:129, :]
            o = (slot * 4 + r) * 128
            mixb[o : o + 128, :] = mix.astype(BF16)

    conv(0, 32, 0, 0)
    lin = dot(mixb[0:512, :], pw_ref[1], 1, 1)
    for r in range(4):
        squash = jnp.tanh(lin[r * 128 : r * 128 + 128] + b_ref[1:2, :])
        slope1[r * 128 : r * 128 + 128, :] = 1.0 - squash * squash
        act = t1[0:128, (r + 1) * 128 : (r + 2) * 128] + squash
        tan2[r * 128 : r * 128 + 128, :] = act.astype(BF16)
    out = dot(wout_ref[...], tan2[0:512, :], 1, 1)
    for r in range(4):
        rows = pl.ds(r, 8, stride=4)
        ns_ref[rows, :] = st_ref[rows, :] + out[:, r * 128 : r * 128 + 128]

    @pl.loop(0, blocks)
    def _(blk):
        @pl.when(has_n)
        def _():
            piece(blk, True).wait_send()
            piece(blk, False).wait_recv()

        @pl.when(has_s)
        def _():
            piece(blk, False).wait_send()
            piece(blk, True).wait_recv()

        pieces = []
        for j in range(BLOCK):
            d = blk * BLOCK + j
            x = field(tg_ref, d * 32, pl.multiple_of(d * 16, 16))
            pieces.append(
                shifted(
                    x,
                    pltpu.roll(ehf[:, 0:128], 32 - d, 1),
                    pltpu.roll(ehf[:, 0:128], 127 - d, 1),
                )
            )
        x3 = jnp.concatenate(pieces, axis=1).astype(BF16)
        base = dot(x3[64:128], w0[...], 0, 0)
        lin = dot(x3, w1[...], 0, 0)
        for j in range(BLOCK):
            rows = slice(j * 128, j * 128 + 128)
            t1[rows, :] = base[rows] + slope0[...] * lin[rows]
        for j in range(BLOCK):
            conv(j * 128, blk * BLOCK + j, j, j)
        lin = dot(mixb[...], pw_ref[1], 1, 1)
        for j in range(BLOCK):
            for r in range(4):
                o = (j * 4 + r) * 128
                v = t1[j * 128 : j * 128 + 128, (r + 1) * 128 : (r + 2) * 128]
                v = v + slope1[r * 128 : r * 128 + 128, :] * lin[o : o + 128]
                tan2[o : o + 128, :] = v.astype(BF16)
        out = dot(wout_ref[...], tan2[...], 1, 1)
        for j in range(BLOCK):
            d = blk * BLOCK + j
            for r in range(4):
                o = (j * 4 + r) * 128
                push[r, pl.ds(d, 8, stride=32), :] = (
                    tg_ref[pl.ds(d * 32 + r, 8, stride=4), :] + out[:, o : o + 128]
                )

    for v in range(8):
        for r in range(4):
            p = push[r, v * 32 : v * 32 + 32, :]
            hi = p.astype(BF16)
            lo = (p - hi.astype(F32)).astype(BF16)
            o = (v * 4 + r) * 128
            pair[:, o : o + 128] = jnp.concatenate([hi, lo], axis=0)
    four = dot(pair[...], pair[...], 1, 1)
    gram = four[0:32, 0:32] + four[0:32, 32:64] + (four[32:64, 0:32] + four[32:64, 32:64])
    gbuf[me] = jnp.concatenate([gram[i * 8 : i * 8 + 8] for i in range(4)], axis=1)

    def gram_copy(i):
        return pltpu.make_async_remote_copy(
            src_ref=gbuf.at[me], dst_ref=gbuf.at[me],
            send_sem=gssem.at[i], recv_sem=grsem.at[i],
            device_id=peer(i),
            device_id_type=pl.DeviceIdType.MESH,
        )

    each(1, n, lambda i: gram_copy(i).start())
    each(1, n, lambda i: gram_copy(i).wait())

    total = jnp.sum(gbuf[...], axis=0) if n <= 16 else lax.fori_loop(1, n, lambda i, g: g + gbuf[i], gbuf[0])
    g = jnp.concatenate([total[:, i * 32 : i * 32 + 32] for i in range(4)], axis=0)
    sub = lax.broadcasted_iota(jnp.int32, (32, 32), 0)
    lan = lax.broadcasted_iota(jnp.int32, (32, 32), 1)
    unit = sub == lan
    a = jnp.concatenate([g, unit.astype(F32)], axis=1)
    row_id = lax.broadcasted_iota(jnp.int32, (32, 1), 0)
    for k in range(32):
        row = a[k : k + 1, :]
        factor = jnp.where(row_id > k, a[:, k : k + 1], 0.0)
        a = a - factor * (row / a[k : k + 1, k : k + 1])
    measure = float(1024 * 4 * n)
    left = jnp.where(unit, a[:, 0:32], 0.0)
    dcol = jnp.sum(left, axis=1, keepdims=True)
    drow = jnp.sum(left, axis=0, keepdims=True)
    inv = a[:, 32:64] * (math.sqrt(measure) / jnp.sqrt(dcol))
    sr_ref[...] = 0.5 * jnp.log(drow) - 0.5 * math.log(measure)
    hi = inv.astype(BF16)
    lo = (inv - hi.astype(F32)).astype(BF16)
    both = jnp.concatenate(
        [jnp.concatenate([hi, hi], axis=1), jnp.concatenate([lo, lo], axis=1)], axis=0
    )
    for c in range(8):
        out = dot(both, pair[:, c * 512 : c * 512 + 512], 1, 0)
        out = out[0:32] + out[32:64]
        for r in range(4):
            fr_ref[pl.ds(c * 4 + r, 32, stride=32), :] = out[:, r * 128 : r * 128 + 128]


def per_device(lats, lons, state, tangents, w_in, w_dw, w_pw, b_pw, w_out):
    n = lats * lons
    vm = pl.BlockSpec(memory_space=pltpu.VMEM)
    stepped, frames, stretch = pl.pallas_call(
        functools.partial(kernel, lats, lons),
        out_shape=(
            jax.ShapeDtypeStruct((32, 128), F32),
            jax.ShapeDtypeStruct((1024, 128), F32),
            jax.ShapeDtypeStruct((1, 32), F32),
        ),
        in_specs=[pl.BlockSpec(memory_space=pltpu.HBM)] * 7,
        out_specs=(vm,) * 3,
        scratch_shapes=[
            pltpu.VMEM((528, 128), BF16), pltpu.VMEM((528, 128), BF16),
            pltpu.VMEM((528, 128), BF16), pltpu.VMEM((528, 128), BF16),
            pltpu.VMEM((64, 256), BF16), pltpu.VMEM((64, 256), BF16),
            pltpu.VMEM((64, 256), F32), pltpu.VMEM((64, 256), F32),
            pltpu.VMEM((64, 768), BF16), pltpu.VMEM((192, 768), BF16),
            pltpu.VMEM((192, 768), F32), pltpu.VMEM((16, 128), F32),
            pltpu.VMEM((128, 768), F32), pltpu.VMEM((512, 128), F32),
            pltpu.VMEM((BLOCK * 128, 768), F32),
            pltpu.VMEM((4, 136, 128), F32), pltpu.VMEM((4, 136, 128), F32),
            pltpu.VMEM((BLOCK * 512, 128), BF16), pltpu.VMEM((BLOCK * 512, 128), BF16),
            pltpu.VMEM((8, 40, 128), F32), pltpu.VMEM((4, 256, 128), F32),
            pltpu.VMEM((n, 8, 128), F32),
            pltpu.VMEM((64, 4096), BF16),
            pltpu.VMEM((32, 128), F32), pltpu.VMEM((1024, 128), F32),
            pltpu.VMEM(w_in.shape[::-1], BF16), pltpu.VMEM((9, 2, 128), BF16),
            pltpu.VMEM(w_pw.shape, BF16), pltpu.VMEM(b_pw.shape, F32),
            pltpu.VMEM(w_out.shape, BF16),
            pltpu.SemaphoreType.DMA((7 + 64 // BLOCK,)), pltpu.SemaphoreType.DMA((7 + 64 // BLOCK,)),
            pltpu.SemaphoreType.DMA((n,)), pltpu.SemaphoreType.DMA((n,)),
            pltpu.SemaphoreType.DMA((7,)),
        ],
        compiler_params=pltpu.CompilerParams(
            collective_id=0, has_side_effects=True, vmem_limit_bytes=60 * 1024 * 1024
        ),
    )(
        state.reshape(32, 128), tangents.reshape(1024, 128),
        w_in.T, w_dw.transpose(2, 0, 1), w_pw, b_pw, w_out,
    )
    return stepped.reshape(state.shape), frames.reshape(tangents.shape), stretch.reshape(32)


def solution(mesh):
    placed = (P("members", "lat", "lon"), P("members", None, "lat", "lon"), P(), P(), P(), P(), P())
    return jax.shard_map(
        functools.partial(per_device, mesh.shape["lat"], mesh.shape["lon"]),
        mesh=mesh,
        in_specs=placed,
        out_specs=(P("members", "lat", "lon"), P("members", None, "lat", "lon"), P("members")),
        check_vma=False,
    )
```

```python
import functools
import math

import jax
import jax.numpy as jnp
from jax import lax
from jax.experimental import pallas as pl
from jax.experimental.pallas import tpu as pltpu
from jax.sharding import PartitionSpec as P

F32 = jnp.float32
BF16 = jnp.bfloat16
BLOCK = 16
HIGH = lax.Precision.HIGHEST


def dot(a, b, ca, cb, precision=None):
    return lax.dot_general(
        a, b, (((ca,), (cb,)), ((), ())), precision=precision, preferred_element_type=F32
    )


def each(lo, hi, body):
    if hi <= 16:
        for i in range(lo, hi):
            body(i)
    else:
        pl.loop(lo, hi)(body)


def moved(tile, src, dst):
    shift = (dst - src) % 128
    return pltpu.roll(tile, shift, 1) if shift else tile


def kernel(
    lats,
    lons,
    st_in, tg_in, win_in, dw_in, pw_in, b_in, wout_in,
    ns_ref, fr_ref, sr_ref,
    send_n, send_s, recv_n, recv_s, eo, eh, eof, ehf,
    w0, w1, wf, kt, slope0, slope1, t1, c0, c2, mixb, tan2, halo, push, gbuf, pair,
    st_ref, tg_ref, win_ref, dw_ref, pw_ref, b_ref, wout_ref,
    ssem, rsem, gssem, grsem, isem,
):
    lat = lax.axis_index("lat")
    lon = lax.axis_index("lon")
    other = 1 - lon
    n = lats * lons
    me = lat * lons + lon
    has_n = lat > 0
    has_s = lat < lats - 1

    fetch = [
        pltpu.make_async_copy(src, dst, isem.at[i])
        for i, (src, dst) in enumerate(
            (
                (tg_in, tg_ref), (st_in, st_ref), (dw_in, dw_ref), (win_in, win_ref),
                (pw_in, pw_ref), (b_in, b_ref), (wout_in, wout_ref),
            )
        )
    ]
    for c in fetch:
        c.start()
    barrier = pltpu.get_barrier_semaphore()

    def peer(i):
        q = me + i
        q = jnp.where(q >= n, q - n, q)
        return {"lat": q // lons, "lon": q % lons}

    def greet(i):
        pl.semaphore_signal(
            barrier, inc=1, device_id=peer(i), device_id_type=pl.DeviceIdType.MESH
        )

    each(1, n, greet)

    lane = lax.broadcasted_iota(jnp.int32, (32, 128), 1)
    fetch[0].wait()
    fetch[1].wait()

    def own_rows(ref, base):
        return [ref[pl.ds(base + r, 8, stride=4), :] for r in range(4)]

    def prep(d, edge):
        r = own_rows(tg_ref, d * 32)
        o = pl.multiple_of(d * 16, 16)
        send_n[pl.ds(o, 16), :] = jnp.concatenate(r[:2], axis=0).astype(BF16)
        send_s[pl.ds(o, 16), :] = jnp.concatenate(r[2:], axis=0).astype(BF16)
        x = jnp.concatenate(r, axis=0)
        for c, col in enumerate((0, 1, 126, 127)):
            rolled = pltpu.roll(x, lax.rem(c * 32 - col + 128 + d, 128), 1)
            edge = jnp.where(lane == c * 32 + d, rolled, edge)
        return edge

    edge = lax.fori_loop(0, 32, prep, jnp.zeros((32, 128), F32), unroll=8)
    r = own_rows(st_ref, 0)
    send_n[512:528, :] = jnp.concatenate(r[:2], axis=0).astype(BF16)
    send_s[512:528, :] = jnp.concatenate(r[2:], axis=0).astype(BF16)
    x = jnp.concatenate(r, axis=0)
    edge2 = jnp.zeros((32, 128), F32)
    for c, col in enumerate((0, 1, 126, 127)):
        edge2 = jnp.where(lane == c, moved(x, col, c), edge2)
    eo[16:48, 0:128] = edge.astype(BF16)
    eo[16:48, 128:256] = edge2.astype(BF16)

    pl.semaphore_wait(barrier, n - 1)

    def remote(i, src, dst, dlat, dlon):
        return pltpu.make_async_remote_copy(
            src_ref=src, dst_ref=dst, send_sem=ssem.at[i], recv_sem=rsem.at[i],
            device_id={"lat": dlat, "lon": dlon},
            device_id_type=pl.DeviceIdType.MESH,
        )

    across = remote(0, eo.at[pl.ds(16, 32)], eh.at[pl.ds(16, 32)], lat, other)
    north = [
        remote(1, eo.at[pl.ds(16, 16)], eh.at[pl.ds(48, 16)], lat - 1, other),
        remote(2, eo.at[pl.ds(16, 16)], eo.at[pl.ds(48, 16)], lat - 1, lon),
        remote(3, send_n.at[pl.ds(512, 16)], recv_s.at[pl.ds(512, 16)], lat - 1, lon),
    ]
    south = [
        remote(4, eo.at[pl.ds(32, 16)], eh.at[pl.ds(0, 16)], lat + 1, other),
        remote(5, eo.at[pl.ds(32, 16)], eo.at[pl.ds(0, 16)], lat + 1, lon),
        remote(6, send_s.at[pl.ds(512, 16)], recv_n.at[pl.ds(512, 16)], lat + 1, lon),
    ]

    def piece(blk, up):
        o = pl.ds(pl.multiple_of(blk * (BLOCK * 16), BLOCK * 16), BLOCK * 16)
        src, dst = (send_n, recv_s) if up else (send_s, recv_n)
        i = 7 + 2 * blk + (0 if up else 1)
        return remote(i, src.at[o], dst.at[o], lat - 1 if up else lat + 1, lon)

    blocks = 32 // BLOCK
    across.start()

    @pl.when(has_n)
    def _():
        for c in north:
            c.start()

    @pl.when(has_s)
    def _():
        for c in south:
            c.start()

    for blk in range(blocks):

        @pl.when(has_n)
        def _():
            piece(blk, True).start()

        @pl.when(has_s)
        def _():
            piece(blk, False).start()

    @pl.when(jnp.logical_not(has_n))
    def _():
        recv_n[...] = jnp.zeros_like(recv_n)
        eo[0:16, :] = jnp.zeros((16, 256), BF16)
        eh[0:16, :] = jnp.zeros((16, 256), BF16)

    @pl.when(jnp.logical_not(has_s))
    def _():
        recv_s[...] = jnp.zeros_like(recv_s)
        eo[48:64, :] = jnp.zeros((16, 256), BF16)
        eh[48:64, :] = jnp.zeros((16, 256), BF16)

    for c in fetch[2:]:
        c.wait()
    win_t = win_ref[...].astype(F32)
    k0 = [dw_ref[t, 0:1, :].astype(F32) for t in range(9)]
    for t in range(9):
        kt[t : t + 1, :] = dw_ref[t, 1:2, :].astype(F32)
    taps = jnp.concatenate([win_t * k0[t] for t in range(9)], axis=0)
    comp = dot(taps, pw_ref[0].astype(F32), 1, 1, HIGH)
    wf[...] = jnp.zeros_like(wf)
    for out in range(6):
        cols = slice(out * 128, out * 128 + 128)
        wf[(out + 1) * 8 : (out + 2) * 8, cols] = win_t
    w0[...] = wf[0:64, :].astype(BF16)
    wf[0:64, :] = jnp.zeros((64, 768), F32)
    for out in range(6):
        cols = slice(out * 128, out * 128 + 128)
        for a in range(3):
            for s in range(3):
                base = s * 64 + (out + a) * 8
                t = 3 * a + s
                wf[base : base + 8, cols] = comp[t * 8 : t * 8 + 8, :]
    w1[...] = wf[...].astype(BF16)

    across.wait()

    @pl.when(has_n)
    def _():
        for c in north:
            c.wait_send()
        for c in south:
            c.wait_recv()

    @pl.when(has_s)
    def _():
        for c in south:
            c.wait_send()
        for c in north:
            c.wait_recv()

    eof[...] = eo[...].astype(F32)
    ehf[...] = eh[...].astype(F32)

    lane64 = lax.broadcasted_iota(jnp.int32, (64, 128), 1)
    own, oth = eof[:, 0:128], ehf[:, 0:128]
    own2, oth2 = eof[:, 128:256], ehf[:, 128:256]
    parts = (
        ((oth, 64), (own, 96), (oth2, 2), (own2, 3)),
        ((oth, 96), (oth, 0), (oth2, 3), (oth2, 0)),
        ((own, 0), (oth, 32), (own2, 0), (oth2, 1)),
    )
    rim = []
    for a, b, c, d in parts:
        v = moved(d[0], d[1], 65)
        v = jnp.where(lane64 < 65, moved(c[0], c[1], 64), v)
        v = jnp.where(lane64 < 64, moved(b[0], b[1], 32), v)
        v = jnp.where(lane64 < 32, moved(a[0], a[1], 0), v)
        rim.append(jnp.where(lane64 < 66, v, 0.0))

    def shifted(x, left, right):
        l = jnp.where(lane64 == 0, left, pltpu.roll(x, 1, 1))
        r = jnp.where(lane64 == 127, right, pltpu.roll(x, 127, 1))
        return jnp.concatenate([l, x, r], axis=0)

    def field(ref, base, o):
        return jnp.concatenate(
            [recv_n[pl.ds(o, 16), :].astype(F32)]
            + own_rows(ref, base)
            + [recv_s[pl.ds(o, 16), :].astype(F32)],
            axis=0,
        )

    bias0 = jnp.concatenate([b_ref[0:1, :]] * 6, axis=1)
    col = lax.broadcasted_iota(jnp.int32, (1, 768), 1)
    keep = jnp.logical_and(
        jnp.logical_or(has_n, col >= 128), jnp.logical_or(has_s, col < 640)
    ).astype(F32)

    x3 = jnp.concatenate([jnp.concatenate(rim, axis=0),
                          shifted(field(st_ref, 0, 512),
                                  moved(oth2, 3, 0), moved(oth2, 0, 127))], axis=1)
    x3 = x3.astype(BF16)
    base = dot(x3[64:128], w0[...], 0, 0)
    lin = dot(x3, w1[...], 0, 0)
    squash = jnp.tanh(lin[128:256] + bias0) * keep
    slope0[...] = keep - squash * squash
    t1[0:128, :] = base[128:256] + squash
    edge_sq = jnp.tanh(lin[64:72] + bias0) * keep
    edge_slope = keep - edge_sq * edge_sq
    edge_act = base[64:72] + edge_sq
    left = base[0:32] + edge_slope[0:1] * lin[0:32]
    right = base[32:64] + edge_slope[1:2] * lin[32:64]
    for r in range(4):
        for side, (b, dirs, act) in enumerate(
            ((0, left, edge_act[0:1]), (2, right, edge_act[1:2]))
        ):
            def tapped(u):
                return sum(
                    kt[3 * a + b : 3 * a + b + 1, :] * u[:, (r + a) * 128 : (r + a) * 128 + 128]
                    for a in range(3)
                )
            i = r * 2 + side
            halo[i, 0:32, :] = tapped(dirs)
            halo[i, 32:33, :] = tapped(act)

    def conv(row0, d, j, slot):
        q = (slot % 2) * 4
        for r in range(4):
            u = [t1[row0 : row0 + 128, (r + a) * 128 : (r + a) * 128 + 128] for a in range(3)]
            tap = lambda b: sum(kt[3 * a + b : 3 * a + b + 1, :] * u[a] for a in range(3))
            c0[q + r, 8:136, :] = tap(0)
            c0[q + r, 7:8, :] = halo[r * 2, pl.ds(d, 1), :]
            c2[q + r, 0:128, :] = tap(2)
            c2[q + r, 128:129, :] = halo[r * 2 + 1, pl.ds(d, 1), :]
            mix = tap(1) + c0[q + r, 7:135, :] + c2[q + r, 1:129, :]
            o = (slot * 4 + r) * 128
            mixb[o : o + 128, :] = mix.astype(BF16)

    conv(0, 32, 0, 0)
    lin = dot(mixb[0:512, :], pw_ref[1], 1, 1)
    for r in range(4):
        squash = jnp.tanh(lin[r * 128 : r * 128 + 128] + b_ref[1:2, :])
        slope1[r * 128 : r * 128 + 128, :] = 1.0 - squash * squash
        act = t1[0:128, (r + 1) * 128 : (r + 2) * 128] + squash
        tan2[r * 128 : r * 128 + 128, :] = act.astype(BF16)
    out = dot(wout_ref[...], tan2[0:512, :], 1, 1)
    for r in range(4):
        rows = pl.ds(r, 8, stride=4)
        ns_ref[rows, :] = st_ref[rows, :] + out[:, r * 128 : r * 128 + 128]

    @pl.loop(0, blocks)
    def _(blk):
        @pl.when(has_n)
        def _():
            piece(blk, True).wait_send()
            piece(blk, False).wait_recv()

        @pl.when(has_s)
        def _():
            piece(blk, False).wait_send()
            piece(blk, True).wait_recv()

        pieces = []
        for j in range(BLOCK):
            d = blk * BLOCK + j
            x = field(tg_ref, d * 32, pl.multiple_of(d * 16, 16))
            pieces.append(
                shifted(
                    x,
                    pltpu.roll(ehf[:, 0:128], 32 - d, 1),
                    pltpu.roll(ehf[:, 0:128], 127 - d, 1),
                )
            )
        x3 = jnp.concatenate(pieces, axis=1).astype(BF16)
        base = dot(x3[64:128], w0[...], 0, 0)
        lin = dot(x3, w1[...], 0, 0)
        for j in range(BLOCK):
            rows = slice(j * 128, j * 128 + 128)
            t1[rows, :] = base[rows] + slope0[...] * lin[rows]
        for j in range(BLOCK):
            conv(j * 128, blk * BLOCK + j, j, j)
        lin = dot(mixb[...], pw_ref[1], 1, 1)
        for j in range(BLOCK):
            for r in range(4):
                o = (j * 4 + r) * 128
                v = t1[j * 128 : j * 128 + 128, (r + 1) * 128 : (r + 2) * 128]
                v = v + slope1[r * 128 : r * 128 + 128, :] * lin[o : o + 128]
                tan2[o : o + 128, :] = v.astype(BF16)
        out = dot(wout_ref[...], tan2[...], 1, 1)
        for j in range(BLOCK):
            d = blk * BLOCK + j
            for r in range(4):
                o = (j * 4 + r) * 128
                push[r, pl.ds(d, 8, stride=32), :] = (
                    tg_ref[pl.ds(d * 32 + r, 8, stride=4), :] + out[:, o : o + 128]
                )

    for v in range(8):
        for r in range(4):
            p = push[r, v * 32 : v * 32 + 32, :]
            hi = p.astype(BF16)
            lo = (p - hi.astype(F32)).astype(BF16)
            o = (v * 4 + r) * 128
            pair[:, o : o + 128] = jnp.concatenate([hi, lo], axis=0)
    four = dot(pair[...], pair[...], 1, 1)
    gram = four[0:32, 0:32] + four[0:32, 32:64] + (four[32:64, 0:32] + four[32:64, 32:64])
    gbuf[me] = jnp.concatenate([gram[i * 8 : i * 8 + 8] for i in range(4)], axis=1)

    def gram_copy(i):
        return pltpu.make_async_remote_copy(
            src_ref=gbuf.at[me], dst_ref=gbuf.at[me],
            send_sem=gssem.at[i], recv_sem=grsem.at[i],
            device_id=peer(i),
            device_id_type=pl.DeviceIdType.MESH,
        )

    each(1, n, lambda i: gram_copy(i).start())
    each(1, n, lambda i: gram_copy(i).wait())

    total = jnp.sum(gbuf[...], axis=0) if n <= 16 else lax.fori_loop(1, n, lambda i, g: g + gbuf[i], gbuf[0])
    g = jnp.concatenate([total[:, i * 32 : i * 32 + 32] for i in range(4)], axis=0)
    sub = lax.broadcasted_iota(jnp.int32, (32, 32), 0)
    lan = lax.broadcasted_iota(jnp.int32, (32, 32), 1)
    unit = sub == lan
    a = jnp.concatenate([g, unit.astype(F32)], axis=1)
    row_id = lax.broadcasted_iota(jnp.int32, (32, 1), 0)
    for k in range(32):
        row = a[k : k + 1, :]
        factor = jnp.where(row_id > k, a[:, k : k + 1], 0.0)
        a = a - factor * (row / a[k : k + 1, k : k + 1])
    measure = float(1024 * 4 * n)
    left = jnp.where(unit, a[:, 0:32], 0.0)
    dcol = jnp.sum(left, axis=1, keepdims=True)
    drow = jnp.sum(left, axis=0, keepdims=True)
    inv = a[:, 32:64] * (math.sqrt(measure) / jnp.sqrt(dcol))
    sr_ref[...] = 0.5 * jnp.log(drow) - 0.5 * math.log(measure)
    hi = inv.astype(BF16)
    lo = (inv - hi.astype(F32)).astype(BF16)
    both = jnp.concatenate(
        [jnp.concatenate([hi, hi], axis=1), jnp.concatenate([lo, lo], axis=1)], axis=0
    )
    for c in range(8):
        out = dot(both, pair[:, c * 512 : c * 512 + 512], 1, 0)
        out = out[0:32] + out[32:64]
        for r in range(4):
            fr_ref[pl.ds(c * 4 + r, 32, stride=32), :] = out[:, r * 128 : r * 128 + 128]


def per_device(lats, lons, state, tangents, w_in, w_dw, w_pw, b_pw, w_out):
    n = lats * lons
    vm = pl.BlockSpec(memory_space=pltpu.VMEM)
    stepped, frames, stretch = pl.pallas_call(
        functools.partial(kernel, lats, lons),
        out_shape=(
            jax.ShapeDtypeStruct((32, 128), F32),
            jax.ShapeDtypeStruct((1024, 128), F32),
            jax.ShapeDtypeStruct((1, 32), F32),
        ),
        in_specs=[pl.BlockSpec(memory_space=pltpu.HBM)] * 7,
        out_specs=(vm,) * 3,
        scratch_shapes=[
            pltpu.VMEM((528, 128), BF16), pltpu.VMEM((528, 128), BF16),
            pltpu.VMEM((528, 128), BF16), pltpu.VMEM((528, 128), BF16),
            pltpu.VMEM((64, 256), BF16), pltpu.VMEM((64, 256), BF16),
            pltpu.VMEM((64, 256), F32), pltpu.VMEM((64, 256), F32),
            pltpu.VMEM((64, 768), BF16), pltpu.VMEM((192, 768), BF16),
            pltpu.VMEM((192, 768), F32), pltpu.VMEM((16, 128), F32),
            pltpu.VMEM((128, 768), F32), pltpu.VMEM((512, 128), F32),
            pltpu.VMEM((BLOCK * 128, 768), F32),
            pltpu.VMEM((8, 136, 128), F32), pltpu.VMEM((8, 136, 128), F32),
            pltpu.VMEM((BLOCK * 512, 128), BF16), pltpu.VMEM((BLOCK * 512, 128), BF16),
            pltpu.VMEM((8, 40, 128), F32), pltpu.VMEM((4, 256, 128), F32),
            pltpu.VMEM((n, 8, 128), F32),
            pltpu.VMEM((64, 4096), BF16),
            pltpu.VMEM((32, 128), F32), pltpu.VMEM((1024, 128), F32),
            pltpu.VMEM(w_in.shape[::-1], BF16), pltpu.VMEM((9, 2, 128), BF16),
            pltpu.VMEM(w_pw.shape, BF16), pltpu.VMEM(b_pw.shape, F32),
            pltpu.VMEM(w_out.shape, BF16),
            pltpu.SemaphoreType.DMA((7 + 64 // BLOCK,)), pltpu.SemaphoreType.DMA((7 + 64 // BLOCK,)),
            pltpu.SemaphoreType.DMA((n,)), pltpu.SemaphoreType.DMA((n,)),
            pltpu.SemaphoreType.DMA((7,)),
        ],
        compiler_params=pltpu.CompilerParams(
            collective_id=0, has_side_effects=True, vmem_limit_bytes=60 * 1024 * 1024
        ),
    )(
        state.reshape(32, 128), tangents.reshape(1024, 128),
        w_in.T, w_dw.transpose(2, 0, 1), w_pw, b_pw, w_out,
    )
    return stepped.reshape(state.shape), frames.reshape(tangents.shape), stretch.reshape(32)


def solution(mesh):
    placed = (P("members", "lat", "lon"), P("members", None, "lat", "lon"), P(), P(), P(), P(), P())
    return jax.shard_map(
        functools.partial(per_device, mesh.shape["lat"], mesh.shape["lon"]),
        mesh=mesh,
        in_specs=placed,
        out_specs=(P("members", "lat", "lon"), P("members", None, "lat", "lon"), P("members")),
        check_vma=False,
    )
```
